128 devices in a mesh: dp: 64 (over y, z, x), mp: 2 (over core).
Axes of the slice: x: 4, y: 4, z: 4, core: 2. Of those that a mesh axis runs over, the one named last changes fastest.
Arguments:
- grads: bfloat16 [16384, 6144], P('dp', 'mp'), may hold values from -0.796875 to 0.796875
- slot_block: int32 [128], replicated, may hold values from -1 to 95, as said below
- left_stats: float32 [128, 1024, 1024], P('dp', 'mp'), may hold values from -6 to 6
- right_stats: float32 [128, 1024, 1024], P('dp', 'mp'), may hold values from -6 to 6
- left_root: bfloat16 [128, 1024, 1024], P('dp', 'mp'), may hold values from -0.59765625 to 0.59765625
- right_root: bfloat16 [128, 1024, 1024], P('dp', None, 'mp'), may hold values from -0.59765625 to 0.59765625
Outputs:
- direction: bfloat16 [16384, 6144], P('dp', 'mp')
- new_left: float32 [128, 1024, 1024], P('dp', 'mp')
- new_right: float32 [128, 1024, 1024], P('dp', 'mp')
The draws below stay inside these ranges and needn't reach their ends.
Inputs may be any that keep to these rules, and one draw needn't show every extreme that they name: slot_block[s] names the block whose statistics sit in slot s, or -1 for an empty slot; every block 0 to 95 stands in exactly one slot; slots k * 2 to k * 2 + 1 lie on dp index k, and some dp index holds 2 blocks.
All inputs are finite; a program needn't handle non-finite values.
Results may differ from the reference program's by a relative error of at most 0.005.
Values may be sent and summed in bfloat16 or wider, within the bound.
A program may use at most 128 MiB of HBM per device.

```python
import jax
import jax.numpy as jnp
from jax import lax

BS = 1024
BCOL = 6
NBLK = 96
ROWS = 16384
WIDTH = 6144
SLOTS = 128


def draw_slot_block(key, part):
    key = jax.random.fold_in(key, 7)
    order = jax.random.permutation(key, SLOTS)
    return jnp.where(order < NBLK, order, -1).astype(jnp.int32)


def levels(rng, extent, cuts, least, high):
    factor_of = 1.0
    for axis_at, blocks in cuts:
        heights = jax.random.uniform(jax.random.fold_in(jax.random.fold_in(rng, 6), axis_at), (blocks,), jnp.float32, least / len(cuts), high / len(cuts))
        factor_of = factor_of * jnp.repeat(jnp.exp(heights), extent[axis_at] // blocks).reshape((-1,) + (1,) * (len(extent) - 1 - axis_at))
    return factor_of


def normal_values(rng, extent, spread, limit, pieces=(), kind=jnp.bfloat16):
    loudness = levels(rng, extent, pieces, -0.22, 0.18) if pieces else 1.0
    drawn = jax.random.normal(rng, extent, jnp.float32) * spread * loudness
    return jnp.minimum(jnp.maximum(drawn, -limit), limit).astype(kind)


def setup_inputs(seed: int = 0) -> dict:
    keys = jax.random.split(jax.random.key(seed), 7)
    return {
        "grads": normal_values(keys[0], (ROWS, WIDTH), 0.1, 0.796875, ((0, 64), (1, 2))),
        "slot_block": draw_slot_block(jax.random.fold_in(keys[6], 71), 0),
        "left_stats": normal_values(keys[2], (SLOTS, BS, BS), 1.0, 6.0, ((0, 64), (1, 2)), jnp.float32),
        "right_stats": normal_values(keys[3], (SLOTS, BS, BS), 1.0, 6.0, ((0, 64), (1, 2)), jnp.float32),
        "left_root": normal_values(keys[4], (SLOTS, BS, BS), 0.1, 0.59765625, ((0, 64), (1, 2))),
        "right_root": normal_values(keys[5], (SLOTS, BS, BS), 0.1, 0.59765625, ((0, 64), (2, 2))),
    }


beta_decay = 0.9


def reference(grads, slot_block, left_stats, right_stats, left_root, right_root):
    filled = slot_block >= 0
    block_ids = jnp.maximum(slot_block, 0).astype(jnp.int32)

    def per_slot(items):
        block_id, present, stats_left, stats_right, root_left, root_right = items
        row_start = ((block_id // BCOL) * BS).astype(jnp.int32)
        col_start = ((block_id % BCOL) * BS).astype(jnp.int32)
        picked = lax.dynamic_slice(grads, (row_start, col_start), (BS, BS))
        slot_grad = jnp.where(present, picked, jnp.zeros_like(picked)).astype(jnp.float32)
        gram_left = jnp.dot(slot_grad, slot_grad.T, preferred_element_type=jnp.float32)
        gram_right = jnp.dot(slot_grad.T, slot_grad, preferred_element_type=jnp.float32)
        updated_left = beta_decay * stats_left + (1.0 - beta_decay) * gram_left
        updated_right = beta_decay * stats_right + (1.0 - beta_decay) * gram_right
        left_part = jnp.dot(root_left.astype(jnp.float32), slot_grad, preferred_element_type=jnp.float32).astype(jnp.bfloat16)
        slot_dir = jnp.dot(left_part.astype(jnp.float32), root_right.astype(jnp.float32), preferred_element_type=jnp.float32).astype(jnp.bfloat16)
        return updated_left, updated_right, slot_dir

    new_left, new_right, slot_dir = lax.map(per_slot, (block_ids, filled, left_stats, right_stats, left_root, right_root))
    slot_ids = jnp.arange(slot_block.shape[0], dtype=jnp.int32)
    block_range = jnp.arange(NBLK, dtype=jnp.int32)
    matches = slot_block[None, :] == block_range[:, None]
    position = jnp.sum(jnp.where(matches, slot_ids[None, :], 0), axis=1).astype(jnp.int32)
    tiles = slot_dir[position]
    block_rows = NBLK // BCOL
    direction = tiles.reshape(block_rows, BCOL, BS, BS).transpose(0, 2, 1, 3).reshape(block_rows * BS, BCOL * BS)
    return direction, new_left, new_right
```

```python
import functools

import jax
import jax.numpy as jnp
from jax import lax
from jax.experimental import pallas as pl
from jax.experimental.pallas import tpu as pltpu
from jax.sharding import PartitionSpec as P

MESH = pl.DeviceIdType.MESH
KEEP = 0.9
SIDE = 4
CHIPS = SIDE**3
PLANE = SIDE**2
BS = 1024
HALF = 512
QUARTER = 256
BLOCKS = 96
SLOTS = 128
SLIVER = 16
CHUNKS = 2
W = HALF // CHUNKS


def negated(offset):
    return tuple(-v % SIDE for v in offset)


def rotated(offset, by):
    return tuple(offset[(i - by) % 3] for i in range(3))


def cube_order():
    order = []
    for a in (1, 3):
        for b in (1, 3):
            order += [(1, a, b), negated((1, a, b))]
    order.append((2, 2, 2))
    for by in range(3):
        for a in (1, 3):
            for offset in (rotated((1, a, 2), by), rotated((1, a, 0), by)):
                order += [offset, negated(offset)]
        for offset in (rotated((1, 2, 2), by), rotated((1, 0, 0), by)):
            order += [offset, negated(offset)]
        order += [rotated((2, 2, 0), by), rotated((0, 0, 2), by)]
    for start in ((1, 2, 0), (1, 0, 2)):
        for by in range(3):
            offset = rotated(start, by)
            order += [offset, negated(offset)]
    return order


def plane_order():
    order = []
    for offset in ((1, 1, 0), (1, 3, 0), (1, 2, 0), (2, 1, 0), (1, 0, 0), (0, 1, 0)):
        order += [offset, negated(offset)]
    return order[:4] + [(2, 2, 0)] + order[4:] + [(2, 0, 0), (0, 2, 0)]


def kernel(
    ids, pos, grads, left_stats, right_stats, left_root, right_root,
    direction, new_left, new_right,
    window, spread, routed, block, left, right, part, result, back, chosen, final, sum_left, sum_right,
    load_sem, store_sem, local_sem, send_sem, recv_sem, line_sem,
):
    dp, me = lax.axis_index("dp"), lax.axis_index("mp")
    y, z, x = dp // PLANE, (dp // SIDE) % SIDE, dp % SIDE
    other = 1 - me
    strip = y * SIDE + z
    my_rows = pl.ds(pl.multiple_of(x * QUARTER + strip * SLIVER, SLIVER), SLIVER)

    def chip(offset):
        a, b, c = (y + offset[0]) % SIDE, (z + offset[1]) % SIDE, (x + offset[2]) % SIDE
        return (a * SIDE + b) * SIDE + c, a * SIDE + b, c

    def cols(core, c):
        return pl.ds(pl.multiple_of(core * HALF + c * W, 128), W)

    def remote(src, dst, sem, device):
        return pltpu.make_async_remote_copy(
            src_ref=src, dst_ref=dst, send_sem=send_sem.at[sem], recv_sem=recv_sem.at[sem],
            device_id=device, device_id_type=MESH,
        )

    P1, P2, P3, P4, LP, GX, LX = (CHUNKS * i for i in range(7))

    loads = [
        pltpu.make_async_copy(grads.at[:, pl.ds(j * BS, BS)], window.at[j], load_sem.at[j]) for j in range(3)
    ]
    my_half = pl.ds(pl.multiple_of(me * HALF, HALF), HALF)
    load_left = pltpu.make_async_copy(left_root, left.at[:, my_half, :], load_sem.at[3])
    load_right = pltpu.make_async_copy(right_root, right, load_sem.at[4])
    load_sl = pltpu.make_async_copy(left_stats, sum_left, load_sem.at[5])
    load_sr = pltpu.make_async_copy(right_stats, sum_right, load_sem.at[6])
    for load in loads:
        load.start()

    barrier = pltpu.get_barrier_semaphore()
    greeted = 0
    for offset in plane_order():
        for core in (me, other):
            pl.semaphore_signal(barrier, inc=1, device_id=(chip(offset)[0], core), device_id_type=MESH)
            greeted += 1
    line = [(chip((0, 0, c))[0], me) for c in (1, 2, 3)]
    for device in [(dp, other)] + line:
        pl.semaphore_signal(barrier, inc=1, device_id=device, device_id_type=MESH)
        greeted += 1
    load_left.start()
    load_right.start()
    load_sl.start()
    load_sr.start()
    for c in range(CHUNKS):
        spread[c][BLOCKS] = jnp.zeros((SLIVER, W), jnp.bfloat16)
    pl.semaphore_wait(barrier, greeted)
    for device in line:
        pl.semaphore_signal(line_sem, inc=1, device_id=device, device_id_type=MESH)

    for load in loads:
        load.wait()
    mine = pl.ds(strip * 6 + me * 3, 3)
    locals_ = []
    for c in range(CHUNKS):
        for offset in plane_order() + [(0, 0, 0)]:
            to, to_strip, _ = chip(offset)
            rows = pl.ds(pl.multiple_of(to_strip * SLIVER, SLIVER), SLIVER)
            for core in (me, other):
                src, dst = window.at[:, rows, cols(core, c)], spread[c].at[mine]
                if any(offset) or core is other:
                    remote(src, dst, P1 + c, (to, core)).start()
                else:
                    copy = pltpu.make_async_copy(src, dst, local_sem.at[P1 + c])
                    copy.start()
                    locals_.append(copy)

    load_left.wait()
    send_left = remote(left.at[:, my_half, :], left.at[:, my_half, :], LX, (dp, other))
    send_left.start()

    pl.semaphore_wait(line_sem, 3)
    routes = []
    for c in range(CHUNKS):
        remote(spread[c].at[pl.ds(0, 93)], spread[c].at[pl.ds(0, 93)], P1 + c, (dp, other)).wait_recv()
        locals_[c].wait()

        def pick(slot, _):
            routed[c, slot] = spread[c][ids[slot]]
            return 0

        lax.fori_loop(0, SLOTS, pick, 0, unroll=8)
        for offset in cube_order():
            to, _, _ = chip(offset)
            remote(
                routed.at[c, pl.ds(2 * to, 2)], block.at[:, my_rows, cols(me, c)], P2 + c, (to, me)
            ).start()
        copy = pltpu.make_async_copy(
            routed.at[c, pl.ds(2 * dp, 2)], block.at[:, my_rows, cols(me, c)], local_sem.at[P2 + c]
        )
        copy.start()
        routes.append(copy)

    load_right.wait()
    exchanges = []
    for c in range(CHUNKS):
        remote(routed.at[c, pl.ds(0, 126)], routed.at[c, pl.ds(0, 126)], P2 + c, (dp, other)).wait_recv()
        routes[c].wait()
        here = cols(me, c)
        send_block = remote(block.at[:, :, here], block.at[:, :, here], GX + c, (dp, other))
        send_block.start()
        if c == 0:
            send_left.wait_recv()

        def left_tile(i, _):
            s, r = i // 4, i % 4
            rows = pl.ds(pl.multiple_of(r * 256, 256), 256)
            part[s, rows, here] = jnp.dot(
                left[s, rows, :], block[s, :, here], preferred_element_type=jnp.float32
            ).astype(jnp.bfloat16)
            return 0

        lax.fori_loop(0, 8, left_tile, 0)
        send_part = remote(part.at[:, :, here], part.at[:, :, here], LP + c, (dp, other))
        send_part.start()
        exchanges += [send_part, send_block]
    for c in range(CHUNKS):
        exchanges[2 * c].wait_recv()

    homes = []
    for c in range(CHUNKS):
        def dir_tile(i, _):
            s, r = i // 4, i % 4
            rows = pl.ds(pl.multiple_of(r * 256, 256), 256)
            result[s, rows, pl.ds(c * W, W)] = jnp.dot(
                part[s, rows, :], right[s, :, pl.ds(c * W, W)], preferred_element_type=jnp.float32
            ).astype(jnp.bfloat16)
            return 0

        lax.fori_loop(0, 8, dir_tile, 0)
        for offset in cube_order():
            to, to_strip, to_x = chip(offset)
            rows = pl.ds(pl.multiple_of(to_x * QUARTER + to_strip * SLIVER, SLIVER), SLIVER)
            remote(
                result.at[:, rows, pl.ds(c * W, W)], back[c].at[pl.ds(2 * dp, 2)], P3 + c, (to, me)
            ).start()
        copy = pltpu.make_async_copy(
            result.at[:, my_rows, pl.ds(c * W, W)], back[c].at[pl.ds(2 * dp, 2)], local_sem.at[P3 + c]
        )
        copy.start()
        homes.append(copy)

    for c in range(CHUNKS):
        exchanges[2 * c + 1].wait_recv()
    load_sl.wait()
    load_sr.wait()

    def gram_left(i, _):
        s, r, n = i // 4, (i // 2) % 2, i % 2
        rows = pl.ds(pl.multiple_of(r * 256, 256), 256)
        own = pl.ds(pl.multiple_of(me * HALF + r * 256, 256), 256)
        to = pl.ds(pl.multiple_of(n * 512, 512), 512)
        gram = lax.dot_general(
            block[s, own, :], block[s, to, :], (((1,), (1,)), ((), ())), preferred_element_type=jnp.float32
        )
        sum_left[s, rows, to] = KEEP * sum_left[s, rows, to] + (1.0 - KEEP) * gram
        return 0

    def gram_right(i, _):
        s, r, n = i // 4, (i // 2) % 2, i % 2
        rows = pl.ds(pl.multiple_of(r * 256, 256), 256)
        own = pl.ds(pl.multiple_of(me * HALF + r * 256, 256), 256)
        to = pl.ds(pl.multiple_of(n * 512, 512), 512)
        gram = lax.dot_general(
            block[s, :, own], block[s, :, to], (((0,), (0,)), ((), ())), preferred_element_type=jnp.float32
        )
        sum_right[s, rows, to] = KEEP * sum_right[s, rows, to] + (1.0 - KEEP) * gram
        return 0

    lax.fori_loop(0, 8, gram_left, 0)
    store_left = pltpu.make_async_copy(sum_left, new_left, store_sem.at[0])
    store_left.start()
    lax.fori_loop(0, 8, gram_right, 0)
    store_right = pltpu.make_async_copy(sum_right, new_right, store_sem.at[1])
    store_right.start()

    ends = []
    for c in range(CHUNKS):
        remote(back[c].at[pl.ds(0, 126)], back[c].at[pl.ds(0, 126)], P3 + c, (dp, other)).wait_recv()
        homes[c].wait()

        def choose(b, _):
            chosen[c, b] = back[c][pos[b]]
            return 0

        lax.fori_loop(0, BLOCKS, choose, 0, unroll=8)
        rows = pl.ds(pl.multiple_of(strip * SLIVER, SLIVER), SLIVER)
        for offset in plane_order() + [(0, 0, 0)]:
            to, to_strip, _ = chip(offset)
            for core in (me, other):
                src, dst = chosen.at[c, pl.ds(to_strip * 6 + core * 3, 3)], final.at[:, rows, cols(me, c)]
                if any(offset) or core is other:
                    remote(src, dst, P4 + c, (to, core)).start()
                else:
                    copy = pltpu.make_async_copy(src, dst, local_sem.at[P4 + c])
                    copy.start()
                    ends.append(copy)
    stores = []
    for c in range(CHUNKS):
        remote(chosen.at[c, pl.ds(0, 93)], chosen.at[c, pl.ds(0, 93)], P4 + c, (dp, other)).wait_recv()
        ends[c].wait()
        for j in range(3):
            for core in range(2):
                at = core * HALF + c * W
                copy = pltpu.make_async_copy(
                    final.at[j, :, pl.ds(at, W)], direction.at[:, pl.ds(j * BS + at, W)],
                    store_sem.at[2 + (c * 3 + j) * 2 + core],
                )
                copy.start()
                stores.append(copy)

    for c in range(CHUNKS):
        remote(spread[c].at[pl.ds(0, 93)], spread[c].at[pl.ds(0, 93)], P1 + c, (dp, other)).wait_send()
        remote(routed.at[c, pl.ds(0, 126)], routed.at[c, pl.ds(0, 126)], P2 + c, (dp, other)).wait_send()
        remote(back[c].at[pl.ds(0, 126)], back[c].at[pl.ds(0, 126)], P3 + c, (dp, other)).wait_send()
        remote(chosen.at[c, pl.ds(0, 93)], chosen.at[c, pl.ds(0, 93)], P4 + c, (dp, other)).wait_send()
    send_left.wait_send()
    for copy in exchanges:
        copy.wait_send()
    for copy in [store_left, store_right] + stores:
        copy.wait()


def on_device(grads, slot_block, left_stats, right_stats, left_root, right_root):
    ids = jnp.where(slot_block >= 0, slot_block, BLOCKS).astype(jnp.int32)
    matches = slot_block[None, :] == jnp.arange(BLOCKS, dtype=jnp.int32)[:, None]
    pos = jnp.sum(jnp.where(matches, jnp.arange(SLOTS, dtype=jnp.int32)[None, :], 0), axis=1)
    bf16 = jnp.bfloat16
    anywhere = pl.BlockSpec(memory_space=pl.ANY)
    scalars = pl.BlockSpec(memory_space=pltpu.SMEM)
    outs = [(grads.shape, bf16), (left_stats.shape, jnp.float32), (right_stats.shape, jnp.float32)]
    return pl.pallas_call(
        kernel,
        out_shape=[jax.ShapeDtypeStruct(*out) for out in outs],
        in_specs=[scalars] * 2 + [anywhere] * 5,
        out_specs=[anywhere] * 3,
        scratch_shapes=[
            pltpu.VMEM((3, QUARTER, BS), bf16),
            [pltpu.VMEM((BLOCKS + 1, SLIVER, W), bf16) for _ in range(CHUNKS)],
            pltpu.VMEM((CHUNKS, SLOTS, SLIVER, W), bf16),
            pltpu.VMEM((2, BS, BS), bf16),
            pltpu.VMEM((2, BS, BS), bf16),
            pltpu.VMEM((2, BS, HALF), bf16),
            pltpu.VMEM((2, BS, BS), bf16),
            pltpu.VMEM((2, BS, HALF), bf16),
            [pltpu.VMEM((SLOTS, SLIVER, W), bf16) for _ in range(CHUNKS)],
            pltpu.VMEM((CHUNKS, BLOCKS, SLIVER, W), bf16),
            pltpu.VMEM((3, QUARTER, BS), bf16),
            pltpu.VMEM((2, HALF, BS), jnp.float32),
            pltpu.VMEM((2, HALF, BS), jnp.float32),
            pltpu.SemaphoreType.DMA((7,)),
            pltpu.SemaphoreType.DMA((2 + 6 * CHUNKS,)),
            pltpu.SemaphoreType.DMA((4 * CHUNKS,)),
            pltpu.SemaphoreType.DMA((7 * CHUNKS,)),
            pltpu.SemaphoreType.DMA((7 * CHUNKS,)),
            pltpu.SemaphoreType.REGULAR,
        ],
        compiler_params=pltpu.CompilerParams(
            collective_id=0, has_side_effects=True, vmem_limit_bytes=60 * 2**20
        ),
    )(ids, pos, grads, left_stats, right_stats, left_root, right_root)


def solution(mesh):
    return jax.shard_map(
        on_device,
        mesh=mesh,
        in_specs=(
            P("dp", "mp"),
            P(),
            P("dp", "mp", None),
            P("dp", "mp", None),
            P("dp", "mp", None),
            P("dp", None, "mp"),
        ),
        out_specs=(P("dp", "mp"), P("dp", "mp", None), P("dp", "mp", None)),
        check_vma=False,
    )
```

```python
import functools

import jax
import jax.numpy as jnp
from jax import lax
from jax.experimental import pallas as pl
from jax.experimental.pallas import tpu as pltpu
from jax.sharding import PartitionSpec as P

MESH = pl.DeviceIdType.MESH
KEEP = 0.9
SIDE = 4
CHIPS = SIDE**3
PLANE = SIDE**2
BS = 1024
HALF = 512
QUARTER = 256
BLOCKS = 96
SLOTS = 128
SLIVER = 16
CHUNKS = 2
W = HALF // CHUNKS


def negated(offset):
    return tuple(-v % SIDE for v in offset)


def rotated(offset, by):
    return tuple(offset[(i - by) % 3] for i in range(3))


def cube_order():
    order = []
    for a in (1, 3):
        for b in (1, 3):
            order += [(1, a, b), negated((1, a, b))]
    order.append((2, 2, 2))
    for by in range(3):
        for a in (1, 3):
            for offset in (rotated((1, a, 2), by), rotated((1, a, 0), by)):
                order += [offset, negated(offset)]
        for offset in (rotated((1, 2, 2), by), rotated((1, 0, 0), by)):
            order += [offset, negated(offset)]
        order += [rotated((2, 2, 0), by), rotated((0, 0, 2), by)]
    for start in ((1, 2, 0), (1, 0, 2)):
        for by in range(3):
            offset = rotated(start, by)
            order += [offset, negated(offset)]
    return order


def plane_order():
    order = []
    for offset in ((1, 1, 0), (1, 3, 0), (1, 2, 0), (2, 1, 0), (1, 0, 0), (0, 1, 0)):
        order += [offset, negated(offset)]
    return order[:4] + [(2, 2, 0)] + order[4:] + [(2, 0, 0), (0, 2, 0)]


def kernel(
    ids, grads, left_stats, right_stats, left_root, right_root,
    direction, new_left, new_right,
    window, spread, routed, block, left, right, part, result, back, chosen, table, places,
    load_sem, local_sem, send_sem, recv_sem, line_sem,
):
    dp, me = lax.axis_index("dp"), lax.axis_index("mp")
    y, z, x = dp // PLANE, (dp // SIDE) % SIDE, dp % SIDE
    other = 1 - me
    strip = y * SIDE + z
    my_rows = pl.ds(pl.multiple_of(x * QUARTER + strip * SLIVER, SLIVER), SLIVER)
    my_half = pl.ds(pl.multiple_of(me * HALF, HALF), HALF)
    drain = []

    def chip(offset):
        a, b, c = (y + offset[0]) % SIDE, (z + offset[1]) % SIDE, (x + offset[2]) % SIDE
        return (a * SIDE + b) * SIDE + c, a * SIDE + b, c

    def cols(core, c):
        return pl.ds(pl.multiple_of(core * HALF + c * W, 128), W)

    def remote(src, dst, sem, device):
        return pltpu.make_async_remote_copy(
            src_ref=src, dst_ref=dst, send_sem=send_sem.at[sem], recv_sem=recv_sem.at[sem],
            device_id=device, device_id_type=MESH,
        )

    def many(pieces, sem):
        span = routed.at[0, pl.ds(0, pieces)]
        return remote(span, span, sem, (dp, other))

    P1, P3, P4 = 0, CHUNKS, 2 * CHUNKS
    P2, PX, GX, LX = 3 * CHUNKS, 3 * CHUNKS + 2, 3 * CHUNKS + 4, 3 * CHUNKS + 6

    loads = [
        pltpu.make_async_copy(grads.at[:, pl.ds(j * BS, BS)], window.at[j], load_sem.at[j]) for j in range(3)
    ]
    load_left = pltpu.make_async_copy(left_root, left.at[:, my_half, :], load_sem.at[3])
    load_right = pltpu.make_async_copy(right_root, right, load_sem.at[4])
    load_sl = pltpu.make_async_copy(left_stats, new_left, load_sem.at[5])
    load_sr = pltpu.make_async_copy(right_stats, new_right, load_sem.at[6])
    for load in loads:
        load.start()

    barrier = pltpu.get_barrier_semaphore()
    greeted = 0
    for offset in plane_order():
        for core in (me, other):
            pl.semaphore_signal(barrier, inc=1, device_id=(chip(offset)[0], core), device_id_type=MESH)
            greeted += 1
    line = [(chip((0, 0, c))[0], me) for c in (1, 2, 3)]
    for device in [(dp, other)] + line:
        pl.semaphore_signal(barrier, inc=1, device_id=device, device_id_type=MESH)
        greeted += 1
    load_left.start()
    load_right.start()
    load_sl.start()
    load_sr.start()
    for c in range(CHUNKS):
        spread[c][BLOCKS] = jnp.zeros((SLIVER, W), jnp.bfloat16)
    pl.semaphore_wait(barrier, greeted)
    for device in line:
        pl.semaphore_signal(line_sem, inc=1, device_id=device, device_id_type=MESH)
    for load in loads:
        load.wait()
    mine = pl.ds(strip * 6 + me * 3, 3)
    kept = []
    for c in range(CHUNKS):
        for offset in plane_order() + [(0, 0, 0)]:
            to, to_strip, _ = chip(offset)
            rows = pl.ds(pl.multiple_of(to_strip * SLIVER, SLIVER), SLIVER)
            for core in (me, other):
                src, dst = window.at[:, rows, cols(core, c)], spread[c].at[mine]
                if any(offset) or core is other:
                    remote(src, dst, P1 + c, (to, core)).start()
                else:
                    kept.append(pltpu.make_async_copy(src, dst, local_sem.at[P1 + c]))
                    kept[-1].start()
        drain.append(many(93, P1 + c))

    load_left.wait()
    send_left = remote(left.at[:, my_half, :], left.at[:, my_half, :], LX, (dp, other))
    send_left.start()
    drain.append(send_left)

    lanes = lax.broadcasted_iota(jnp.int32, (8, SLOTS), 1)

    def seat(slot, seats):
        return jnp.where(lanes == ids[slot], slot, seats)

    table[...] = lax.fori_loop(0, SLOTS, seat, jnp.zeros((8, SLOTS), jnp.int32), unroll=8)
    fetch = pltpu.make_async_copy(table, places, load_sem.at[7])
    fetch.start()

    pl.semaphore_wait(line_sem, 3)

    def pick(c):
        many(93, P1 + c).wait_recv()
        kept[c].wait()

        def one(slot, _):
            held = ids[slot]
            routed[c, slot] = spread[c][jnp.where(held < 0, BLOCKS, held)]
            return 0

        lax.fori_loop(0, SLOTS, one, 0, unroll=8)

    arrivals = {}

    def route(c, s):
        for offset in cube_order():
            to, _, _ = chip(offset)
            remote(routed.at[c, 2 * to + s], block.at[s, my_rows, cols(me, c)], P2 + s, (to, me)).start()
        arrivals[c, s] = pltpu.make_async_copy(
            routed.at[c, 2 * dp + s], block.at[s, my_rows, cols(me, c)], local_sem.at[2 * CHUNKS + 2 * c + s]
        )
        arrivals[c, s].start()

    for c in range(CHUNKS):
        pick(c)
        route(c, 0)
    for c in range(CHUNKS):
        route(c, 1)
    fetch.wait()
    drain += [many(63 * CHUNKS, P2 + s) for s in range(2)]

    own = pl.ds(pl.multiple_of(me * HALF, HALF), HALF)
    exchanges = []

    def arrive(s):
        many(63 * CHUNKS, P2 + s).wait_recv()
        for c in range(CHUNKS):
            arrivals[c, s].wait()
        send_block = remote(block.at[s, :, own], block.at[s, :, own], GX + s, (dp, other))
        send_block.start()
        exchanges.append(send_block)
        drain.append(send_block)
        if s == 0:
            send_left.wait_recv()

        def left_tile(r, _):
            rows = pl.ds(pl.multiple_of(r * 256, 256), 256)
            part[s, rows, own] = jnp.dot(
                left[s, rows, :], block[s, :, own], preferred_element_type=jnp.float32
            ).astype(jnp.bfloat16)
            return 0

        lax.fori_loop(0, 4, left_tile, 0)
        send_part = remote(part.at[s, :, own], part.at[s, :, own], PX + s, (dp, other))
        send_part.start()
        drain.append(send_part)
        return send_part

    homes = {}

    def give_back(s, c):
        def dir_tile(r, _):
            rows = pl.ds(pl.multiple_of(r * 256, 256), 256)
            result[s, rows, pl.ds(c * W, W)] = jnp.dot(
                part[s, rows, :], right[s, :, pl.ds(c * W, W)], preferred_element_type=jnp.float32
            ).astype(jnp.bfloat16)
            return 0

        lax.fori_loop(0, 4, dir_tile, 0)
        for offset in cube_order():
            to, to_strip, to_x = chip(offset)
            rows = pl.ds(pl.multiple_of(to_x * QUARTER + to_strip * SLIVER, SLIVER), SLIVER)
            remote(result.at[s, rows, pl.ds(c * W, W)], back[c].at[2 * dp + s], P3 + c, (to, me)).start()
        homes[c, s] = pltpu.make_async_copy(
            result.at[s, my_rows, pl.ds(c * W, W)], back[c].at[2 * dp + s], local_sem.at[4 * CHUNKS + 2 * c + s]
        )
        homes[c, s].start()

    load_right.wait()
    for s in range(2):
        arrive(s).wait_recv()
        for c in range(CHUNKS):
            give_back(s, c)
    for copy in exchanges:
        copy.wait_recv()
    drain += [many(126, P3 + c) for c in range(CHUNKS)]

    load_sl.wait()
    load_sr.wait()

    def gram(i, total, axis):
        s, r, n = i // 4, (i // 2) % 2, i % 2
        rows = pl.ds(pl.multiple_of(r * 256, 256), 256)
        here = pl.ds(pl.multiple_of(me * HALF + r * 256, 256), 256)
        to = pl.ds(pl.multiple_of(n * 512, 512), 512)
        pair = (block[s, here, :], block[s, to, :]) if axis else (block[s, :, here], block[s, :, to])
        product = lax.dot_general(*pair, (((axis,), (axis,)), ((), ())), preferred_element_type=jnp.float32)
        total[s, rows, to] = KEEP * total[s, rows, to] + (1.0 - KEEP) * product

    def gram_left(i, _):
        gram(i, new_left, 1)
        return 0

    def gram_right(i, _):
        gram(i, new_right, 0)
        return 0

    lax.fori_loop(0, 8, gram_left, 0)
    lax.fori_loop(0, 8, gram_right, 0)

    ends = []
    for c in range(CHUNKS):
        many(126, P3 + c).wait_recv()
        for s in range(2):
            homes[c, s].wait()

        def choose(b, _):
            chosen[c, b] = back[c][places[0, b]]
            return 0

        lax.fori_loop(0, BLOCKS, choose, 0, unroll=8)
        rows = pl.ds(pl.multiple_of(strip * SLIVER, SLIVER), SLIVER)
        for offset in plane_order() + [(0, 0, 0)]:
            to, to_strip, _ = chip(offset)
            for core in (me, other):
                for j in range(3):
                    src = chosen.at[c, to_strip * 6 + core * 3 + j]
                    dst = direction.at[rows, pl.ds(pl.multiple_of(j * BS + me * HALF + c * W, 128), W)]
                    if any(offset) or core is other:
                        remote(src, dst, P4 + c, (to, core)).start()
                    else:
                        ends.append(pltpu.make_async_copy(src, dst, local_sem.at[6 * CHUNKS + 3 * c + j]))
                        ends[-1].start()
        drain.append(many(93, P4 + c))
    for c in range(CHUNKS):
        many(93, P4 + c).wait_recv()
    for end in ends:
        end.wait()
    for copy in drain:
        copy.wait_send()


def on_device(grads, slot_block, left_stats, right_stats, left_root, right_root):
    bf16 = jnp.bfloat16
    anywhere = pl.BlockSpec(memory_space=pl.ANY)
    scalars = pl.BlockSpec(memory_space=pltpu.SMEM)
    outs = [(grads.shape, bf16), (left_stats.shape, jnp.float32), (right_stats.shape, jnp.float32)]
    return pl.pallas_call(
        kernel,
        out_shape=[pltpu.VMEM(*out) for out in outs],
        in_specs=[scalars] + [anywhere] * 5,
        out_specs=[pl.BlockSpec(memory_space=pltpu.VMEM)] * 3,
        scratch_shapes=[
            pltpu.VMEM((3, QUARTER, BS), bf16),
            [pltpu.VMEM((BLOCKS + 1, SLIVER, W), bf16) for _ in range(CHUNKS)],
            pltpu.VMEM((CHUNKS, SLOTS, SLIVER, W), bf16),
            pltpu.VMEM((2, BS, BS), bf16),
            pltpu.VMEM((2, BS, BS), bf16),
            pltpu.VMEM((2, BS, HALF), bf16),
            pltpu.VMEM((2, BS, BS), bf16),
            pltpu.VMEM((2, BS, HALF), bf16),
            [pltpu.VMEM((SLOTS, SLIVER, W), bf16) for _ in range(CHUNKS)],
            pltpu.VMEM((CHUNKS, BLOCKS, SLIVER, W), bf16),
            pltpu.VMEM((8, SLOTS), jnp.int32),
            pltpu.SMEM((8, SLOTS), jnp.int32),
            pltpu.SemaphoreType.DMA((8,)),
            pltpu.SemaphoreType.DMA((9 * CHUNKS,)),
            pltpu.SemaphoreType.DMA((3 * CHUNKS + 7,)),
            pltpu.SemaphoreType.DMA((3 * CHUNKS + 7,)),
            pltpu.SemaphoreType.REGULAR,
        ],
        compiler_params=pltpu.CompilerParams(
            collective_id=0, has_side_effects=True, vmem_limit_bytes=50 * 2**20
        ),
    )(slot_block, grads, left_stats, right_stats, left_root, right_root)


def solution(mesh):
    return jax.shard_map(
        on_device,
        mesh=mesh,
        in_specs=(
            P("dp", "mp"),
            P(),
            P("dp", "mp", None),
            P("dp", "mp", None),
            P("dp", "mp", None),
            P("dp", None, "mp"),
        ),
        out_specs=(P("dp", "mp"), P("dp", "mp", None), P("dp", "mp", None)),
        check_vma=False,
    )
```

```python
import functools

import jax
import jax.numpy as jnp
from jax import lax
from jax.experimental import pallas as pl
from jax.experimental.pallas import tpu as pltpu
from jax.sharding import PartitionSpec as P

MESH = pl.DeviceIdType.MESH
KEEP = 0.9
SIDE = 4
CHIPS = SIDE**3
PLANE = SIDE**2
BS = 1024
HALF = 512
QUARTER = 256
BLOCKS = 96
SLOTS = 128
SLIVER = 16
CHUNKS = 2
W = HALF // CHUNKS


def negated(offset):
    return tuple(-v % SIDE for v in offset)


def rotated(offset, by):
    return tuple(offset[(i - by) % 3] for i in range(3))


def cube_order():
    order = []
    for a in (1, 3):
        for b in (1, 3):
            order += [(1, a, b), negated((1, a, b))]
    order.append((2, 2, 2))
    for by in range(3):
        for a in (1, 3):
            for offset in (rotated((1, a, 2), by), rotated((1, a, 0), by)):
                order += [offset, negated(offset)]
        for offset in (rotated((1, 2, 2), by), rotated((1, 0, 0), by)):
            order += [offset, negated(offset)]
        order += [rotated((2, 2, 0), by), rotated((0, 0, 2), by)]
    for start in ((1, 2, 0), (1, 0, 2)):
        for by in range(3):
            offset = rotated(start, by)
            order += [offset, negated(offset)]
    return order


LINES = [(1, 0, 0), (3, 0, 0), (0, 1, 0), (0, 3, 0), (2, 0, 0), (0, 2, 0)]
DIAGONALS = [
    (1, 1, 0), (3, 3, 0), (1, 3, 0), (3, 1, 0), (2, 2, 0), (1, 2, 0), (3, 2, 0), (2, 1, 0), (2, 3, 0)
]


def kernel(
    ids_ref, grads, left_stats, right_stats, left_root, right_root,
    direction, new_left, new_right,
    window, spread, routed, block, left, right, part, result, back, chosen, table, places, ids,
    load_sem, local_sem, send_sem, recv_sem, ready_sem,
):
    dp, me = lax.axis_index("dp"), lax.axis_index("mp")
    y, z, x = dp // PLANE, (dp // SIDE) % SIDE, dp % SIDE
    other = 1 - me
    strip = y * SIDE + z
    my_rows = pl.ds(pl.multiple_of(x * QUARTER + strip * SLIVER, SLIVER), SLIVER)
    my_half = pl.ds(pl.multiple_of(me * HALF, HALF), HALF)
    drain = []

    def chip(offset):
        a, b, c = (y + offset[0]) % SIDE, (z + offset[1]) % SIDE, (x + offset[2]) % SIDE
        return (a * SIDE + b) * SIDE + c, a * SIDE + b, c

    def cols(core, c):
        return pl.ds(pl.multiple_of(core * HALF + c * W, 128), W)

    def remote(src, dst, sem, device):
        return pltpu.make_async_remote_copy(
            src_ref=src, dst_ref=dst, send_sem=send_sem.at[sem], recv_sem=recv_sem.at[sem],
            device_id=device, device_id_type=MESH,
        )

    def many(pieces, sem):
        span = routed.at[0, pl.ds(0, pieces)]
        return remote(span, span, sem, (dp, other))

    def slot_copies(s):
        span = block.at[s, pl.ds(0, 63 * SLIVER), pl.ds(0, HALF)]
        return remote(span, span, P2 + s, (dp, other))

    P1, P3, P4 = 0, CHUNKS, 2 * CHUNKS
    P2, PX, GX, LX = 3 * CHUNKS, 3 * CHUNKS + 2, 3 * CHUNKS + 4, 3 * CHUNKS + 6

    loads = [
        pltpu.make_async_copy(grads.at[:, pl.ds(j * BS, BS)], window.at[j], load_sem.at[j]) for j in range(3)
    ]
    load_left = pltpu.make_async_copy(left_root, left.at[:, my_half, :], load_sem.at[3])
    load_right = pltpu.make_async_copy(right_root, right, load_sem.at[4])
    load_sl = pltpu.make_async_copy(left_stats, new_left, load_sem.at[5])
    load_sr = pltpu.make_async_copy(right_stats, new_right, load_sem.at[6])
    load_ids = pltpu.make_async_copy(ids_ref, ids, load_sem.at[8])
    for load in loads + [load_ids, load_left, load_right, load_sl, load_sr]:
        load.start()

    def tell(devices, sem):
        for device in devices:
            pl.semaphore_signal(sem, inc=1, device_id=device, device_id_type=MESH)

    axes = [[(chip(tuple(n * u for u in unit))[0], me) for n in (1, 2, 3)] for unit in ((1, 0, 0), (0, 1, 0), (0, 0, 1))]
    barrier = pltpu.get_barrier_semaphore()
    tell(axes[0] + axes[1] + axes[2] + [(dp, other)], barrier)
    for c in range(CHUNKS):
        spread[c][BLOCKS] = jnp.zeros((SLIVER, W), jnp.bfloat16)
    pl.semaphore_wait(barrier, 10)

    tell([(dp, other)], ready_sem.at[0])
    for load in loads:
        load.wait()
    mine = pl.ds(strip * 6 + me * 3, 3)

    def scatter(offsets, core):
        for c in range(CHUNKS):
            for offset in offsets:
                to, to_strip, _ = chip(offset)
                rows = pl.ds(pl.multiple_of(to_strip * SLIVER, SLIVER), SLIVER)
                remote(window.at[:, rows, cols(core, c)], spread[c].at[mine], P1 + c, (to, core)).start()

    scatter(LINES, me)
    pl.semaphore_wait(ready_sem.at[0], 1)
    tell(axes[1], ready_sem.at[1])
    scatter([(0, 0, 0)] + LINES, other)
    pl.semaphore_wait(ready_sem.at[1], 3)
    tell(axes[2], ready_sem.at[2])
    for c in range(CHUNKS):
        for offset in DIAGONALS:
            to, to_strip, _ = chip(offset)
            rows = pl.ds(pl.multiple_of(to_strip * SLIVER, SLIVER), SLIVER)
            for core in (me, other):
                remote(window.at[:, rows, cols(core, c)], spread[c].at[mine], P1 + c, (to, core)).start()
    kept = []
    for c in range(CHUNKS):
        rows = pl.ds(pl.multiple_of(strip * SLIVER, SLIVER), SLIVER)
        kept.append(pltpu.make_async_copy(window.at[:, rows, cols(me, c)], spread[c].at[mine], local_sem.at[P1 + c]))
        kept[c].start()
        drain.append(many(93, P1 + c))

    load_left.wait()
    send_left = remote(left.at[:, my_half, :], left.at[:, my_half, :], LX, (dp, other))
    send_left.start()
    drain.append(send_left)

    load_ids.wait()
    lanes = lax.broadcasted_iota(jnp.int32, (8, SLOTS), 1)

    def seat(slot, seats):
        return jnp.where(lanes == ids[slot], slot, seats)

    table[...] = lax.fori_loop(0, SLOTS, seat, jnp.zeros((8, SLOTS), jnp.int32), unroll=8)
    fetch = pltpu.make_async_copy(table, places, load_sem.at[7])
    fetch.start()

    pl.semaphore_wait(ready_sem.at[2], 3)

    def pick(c):
        many(93, P1 + c).wait_recv()
        kept[c].wait()

        def one(slot, _):
            held = ids[slot]
            routed[c, slot] = spread[c][jnp.where(held < 0, BLOCKS, held)]
            return 0

        lax.fori_loop(0, SLOTS, one, 0, unroll=8)

    arrivals = {}

    def route(c, s):
        for offset in cube_order():
            to, _, _ = chip(offset)
            remote(routed.at[c, 2 * to + s], block.at[s, my_rows, cols(me, c)], P2 + s, (to, me)).start()
        arrivals[c, s] = pltpu.make_async_copy(
            routed.at[c, 2 * dp + s], block.at[s, my_rows, cols(me, c)], local_sem.at[2 * CHUNKS + 2 * c + s]
        )
        arrivals[c, s].start()

    for c in range(CHUNKS):
        pick(c)
        route(c, 0)
    for c in range(CHUNKS):
        route(c, 1)
    fetch.wait()
    drain += [slot_copies(s) for s in range(2)]

    own = pl.ds(pl.multiple_of(me * HALF, HALF), HALF)
    exchanges = []

    def arrive(s):
        slot_copies(s).wait_recv()
        for c in range(CHUNKS):
            arrivals[c, s].wait()
        send_block = remote(block.at[s, :, own], block.at[s, :, own], GX + s, (dp, other))
        send_block.start()
        exchanges.append(send_block)
        drain.append(send_block)
        if s == 0:
            send_left.wait_recv()

        def left_tile(r, _):
            rows = pl.ds(pl.multiple_of(r * 256, 256), 256)
            part[s, rows, own] = jnp.dot(
                left[s, rows, :], block[s, :, own], preferred_element_type=jnp.float32
            ).astype(jnp.bfloat16)
            return 0

        lax.fori_loop(0, 4, left_tile, 0)
        send_part = remote(part.at[s, :, own], part.at[s, :, own], PX + s, (dp, other))
        send_part.start()
        drain.append(send_part)
        return send_part

    homes = {}

    def give_back(s, c):
        def dir_tile(r, _):
            rows = pl.ds(pl.multiple_of(r * 256, 256), 256)
            result[s, rows, pl.ds(c * W, W)] = jnp.dot(
                part[s, rows, :], right[s, :, pl.ds(c * W, W)], preferred_element_type=jnp.float32
            ).astype(jnp.bfloat16)
            return 0

        lax.fori_loop(0, 4, dir_tile, 0)
        for offset in cube_order():
            to, to_strip, to_x = chip(offset)
            rows = pl.ds(pl.multiple_of(to_x * QUARTER + to_strip * SLIVER, SLIVER), SLIVER)
            remote(result.at[s, rows, pl.ds(c * W, W)], back[c].at[2 * dp + s], P3 + c, (to, me)).start()
        homes[c, s] = pltpu.make_async_copy(
            result.at[s, my_rows, pl.ds(c * W, W)], back[c].at[2 * dp + s], local_sem.at[4 * CHUNKS + 2 * c + s]
        )
        homes[c, s].start()

    load_right.wait()
    def gram(s, i, total, axis):
        r, n = i // 2, i % 2
        rows = pl.ds(pl.multiple_of(r * 256, 256), 256)
        here = pl.ds(pl.multiple_of(me * HALF + r * 256, 256), 256)
        to = pl.ds(pl.multiple_of(n * 512, 512), 512)
        pair = (block[s, here, :], block[s, to, :]) if axis else (block[s, :, here], block[s, :, to])
        product = lax.dot_general(*pair, (((axis,), (axis,)), ((), ())), preferred_element_type=jnp.float32)
        total[s, rows, to] = KEEP * total[s, rows, to] + (1.0 - KEEP) * product

    def grams(s):
        def both(i, _):
            gram(s, i, new_left, 1)
            gram(s, i, new_right, 0)
            return 0

        lax.fori_loop(0, 4, both, 0)

    for s in range(2):
        arrive(s).wait_recv()
        for c in range(CHUNKS):
            give_back(s, c)
        exchanges[s].wait_recv()
        if s == 0:
            load_sl.wait()
            load_sr.wait()
        grams(s)
    drain += [many(126, P3 + c) for c in range(CHUNKS)]

    ends = []
    for c in range(CHUNKS):
        many(126, P3 + c).wait_recv()
        for s in range(2):
            homes[c, s].wait()

        def choose(b, _):
            chosen[c, b] = back[c][places[0, b]]
            return 0

        lax.fori_loop(0, BLOCKS, choose, 0, unroll=8)
        rows = pl.ds(pl.multiple_of(strip * SLIVER, SLIVER), SLIVER)
        for offset in DIAGONALS + LINES + [(0, 0, 0)]:
            to, to_strip, _ = chip(offset)
            for core in (me, other):
                for j in range(3):
                    src = chosen.at[c, to_strip * 6 + core * 3 + j]
                    dst = direction.at[rows, pl.ds(pl.multiple_of(j * BS + me * HALF + c * W, 128), W)]
                    if any(offset) or core is other:
                        remote(src, dst, P4 + c, (to, core)).start()
                    else:
                        ends.append(pltpu.make_async_copy(src, dst, local_sem.at[6 * CHUNKS + 3 * c + j]))
                        ends[-1].start()
        drain.append(many(93, P4 + c))
    for c in range(CHUNKS):
        many(93, P4 + c).wait_recv()
    for end in ends:
        end.wait()
    for copy in drain:
        copy.wait_send()


def write(a, b, c, a_out, b_out, c_out, sem):
    pairs = [(b, b_out), (c, c_out), (a, a_out)]
    copies = [pltpu.make_async_copy(src, dst, sem.at[i]) for i, (src, dst) in enumerate(pairs)]
    for copy in copies:
        copy.start()
    for copy in copies:
        copy.wait()


def on_device(grads, slot_block, left_stats, right_stats, left_root, right_root):
    bf16 = jnp.bfloat16
    anywhere = pl.BlockSpec(memory_space=pl.ANY)
    outs = [(grads.shape, bf16), (left_stats.shape, jnp.float32), (right_stats.shape, jnp.float32)]
    results = pl.pallas_call(
        kernel,
        out_shape=[pltpu.VMEM(*out) for out in outs],
        in_specs=[anywhere] * 6,
        out_specs=[pl.BlockSpec(memory_space=pltpu.VMEM)] * 3,
        scratch_shapes=[
            pltpu.VMEM((3, QUARTER, BS), bf16),
            [pltpu.VMEM((BLOCKS + 1, SLIVER, W), bf16) for _ in range(CHUNKS)],
            pltpu.VMEM((CHUNKS, SLOTS, SLIVER, W), bf16),
            pltpu.VMEM((2, BS, BS), bf16),
            pltpu.VMEM((2, BS, BS), bf16),
            pltpu.VMEM((2, BS, HALF), bf16),
            pltpu.VMEM((2, BS, BS), bf16),
            pltpu.VMEM((2, BS, HALF), bf16),
            [pltpu.VMEM((SLOTS, SLIVER, W), bf16) for _ in range(CHUNKS)],
            pltpu.VMEM((CHUNKS, BLOCKS, SLIVER, W), bf16),
            pltpu.VMEM((8, SLOTS), jnp.int32),
            pltpu.SMEM((8, SLOTS), jnp.int32),
            pltpu.SMEM((SLOTS,), jnp.int32),
            pltpu.SemaphoreType.DMA((9,)),
            pltpu.SemaphoreType.DMA((9 * CHUNKS,)),
            pltpu.SemaphoreType.DMA((3 * CHUNKS + 7,)),
            pltpu.SemaphoreType.DMA((3 * CHUNKS + 7,)),
            pltpu.SemaphoreType.REGULAR((3,)),
        ],
        compiler_params=pltpu.CompilerParams(
            collective_id=0, has_side_effects=True, vmem_limit_bytes=50 * 2**20
        ),
    )(slot_block, grads, left_stats, right_stats, left_root, right_root)
    return pl.pallas_call(
        write,
        out_shape=[jax.ShapeDtypeStruct(*out) for out in outs],
        in_specs=[anywhere] * 3,
        out_specs=[anywhere] * 3,
        scratch_shapes=[pltpu.SemaphoreType.DMA((3,))],
        compiler_params=pltpu.CompilerParams(vmem_limit_bytes=2**20),
    )(*results)


def solution(mesh):
    return jax.shard_map(
        on_device,
        mesh=mesh,
        in_specs=(
            P("dp", "mp"),
            P(),
            P("dp", "mp", None),
            P("dp", "mp", None),
            P("dp", "mp", None),
            P("dp", None, "mp"),
        ),
        out_specs=(P("dp", "mp"), P("dp", "mp", None), P("dp", "mp", None)),
        check_vma=False,
    )
```

```python
import functools

import jax
import jax.numpy as jnp
from jax import lax
from jax.experimental import pallas as pl
from jax.experimental.pallas import tpu as pltpu
from jax.sharding import PartitionSpec as P

MESH = pl.DeviceIdType.MESH
KEEP = 0.9
SIDE = 4
CHIPS = SIDE**3
PLANE = SIDE**2
BS = 1024
HALF = 512
QUARTER = 256
BLOCKS = 96
SLOTS = 128
SLIVER = 16
CHUNKS = 2
W = HALF // CHUNKS


def negated(offset):
    return tuple(-v % SIDE for v in offset)


def rotated(offset, by):
    return tuple(offset[(i - by) % 3] for i in range(3))


def cube_order():
    order = []
    for a in (1, 3):
        for b in (1, 3):
            order += [(1, a, b), negated((1, a, b))]
    order.append((2, 2, 2))
    for by in range(3):
        for a in (1, 3):
            for offset in (rotated((1, a, 2), by), rotated((1, a, 0), by)):
                order += [offset, negated(offset)]
        for offset in (rotated((1, 2, 2), by), rotated((1, 0, 0), by)):
            order += [offset, negated(offset)]
        order += [rotated((2, 2, 0), by), rotated((0, 0, 2), by)]
    for start in ((1, 2, 0), (1, 0, 2)):
        for by in range(3):
            offset = rotated(start, by)
            order += [offset, negated(offset)]
    return order


LINES = [(1, 0, 0), (3, 0, 0), (0, 1, 0), (0, 3, 0), (2, 0, 0), (0, 2, 0)]
DIAGONALS = [
    (1, 1, 0), (3, 3, 0), (1, 3, 0), (3, 1, 0), (2, 2, 0), (1, 2, 0), (3, 2, 0), (2, 1, 0), (2, 3, 0)
]


def kernel(
    ids_ref, grads, left_stats, right_stats, left_root, right_root,
    direction, new_left, new_right,
    window, spread, routed, block, left, right, part, result, back, chosen, table, places, ids,
    load_sem, local_sem, send_sem, recv_sem, ready_sem,
):
    dp, me = lax.axis_index("dp"), lax.axis_index("mp")
    y, z, x = dp // PLANE, (dp // SIDE) % SIDE, dp % SIDE
    other = 1 - me
    strip = y * SIDE + z
    my_rows = pl.ds(pl.multiple_of(x * QUARTER + strip * SLIVER, SLIVER), SLIVER)
    my_half = pl.ds(pl.multiple_of(me * HALF, HALF), HALF)
    drain = []

    def chip(offset):
        a, b, c = (y + offset[0]) % SIDE, (z + offset[1]) % SIDE, (x + offset[2]) % SIDE
        return (a * SIDE + b) * SIDE + c, a * SIDE + b, c

    def cols(core, c):
        return pl.ds(pl.multiple_of(core * HALF + c * W, 128), W)

    def remote(src, dst, sem, device):
        return pltpu.make_async_remote_copy(
            src_ref=src, dst_ref=dst, send_sem=send_sem.at[sem], recv_sem=recv_sem.at[sem],
            device_id=device, device_id_type=MESH,
        )

    def many(pieces, sem):
        span = routed.at[0, pl.ds(0, pieces)]
        return remote(span, span, sem, (dp, other))

    def slot_copies(s):
        span = block.at[s, pl.ds(0, 63 * SLIVER), pl.ds(0, HALF)]
        return remote(span, span, P2 + s, (dp, other))

    P1, P3, P4 = 0, CHUNKS, 2 * CHUNKS
    P2, PX, GX, LX = 3 * CHUNKS, 3 * CHUNKS + 2, 3 * CHUNKS + 4, 3 * CHUNKS + 6

    loads = [
        pltpu.make_async_copy(grads.at[:, pl.ds(j * BS, BS)], window.at[j], load_sem.at[j]) for j in range(3)
    ]
    load_left = pltpu.make_async_copy(left_root, left.at[:, my_half, :], load_sem.at[3])
    load_right = pltpu.make_async_copy(right_root, right, load_sem.at[4])
    load_sl = pltpu.make_async_copy(left_stats, new_left, load_sem.at[5])
    load_sr = pltpu.make_async_copy(right_stats, new_right, load_sem.at[6])
    load_ids = pltpu.make_async_copy(ids_ref, ids, load_sem.at[8])
    for load in loads:
        load.start()

    def tell(devices, sem):
        for device in devices:
            pl.semaphore_signal(sem, inc=1, device_id=device, device_id_type=MESH)

    axes = [[(chip(tuple(n * u for u in unit))[0], me) for n in (1, 2, 3)] for unit in ((1, 0, 0), (0, 1, 0), (0, 0, 1))]
    barrier = pltpu.get_barrier_semaphore()
    tell(axes[0] + axes[1] + axes[2] + [(dp, other)], barrier)
    for c in range(CHUNKS):
        spread[c][BLOCKS] = jnp.zeros((SLIVER, W), jnp.bfloat16)
    pl.semaphore_wait(barrier, 10)

    tell([(dp, other)], ready_sem.at[0])
    for load in loads:
        load.wait()
    mine = pl.ds(strip * 6 + me * 3, 3)

    def scatter(offsets, core):
        for c in range(CHUNKS):
            for offset in offsets:
                to, to_strip, _ = chip(offset)
                rows = pl.ds(pl.multiple_of(to_strip * SLIVER, SLIVER), SLIVER)
                remote(window.at[:, rows, cols(core, c)], spread[c].at[mine], P1 + c, (to, core)).start()

    scatter(LINES, me)
    for load in (load_ids, load_left, load_right, load_sl, load_sr):
        load.start()
    pl.semaphore_wait(ready_sem.at[0], 1)
    tell(axes[1], ready_sem.at[1])
    scatter([(0, 0, 0)] + LINES, other)
    pl.semaphore_wait(ready_sem.at[1], 3)
    tell(axes[2], ready_sem.at[2])
    for c in range(CHUNKS):
        for offset in DIAGONALS:
            to, to_strip, _ = chip(offset)
            rows = pl.ds(pl.multiple_of(to_strip * SLIVER, SLIVER), SLIVER)
            for core in (me, other):
                remote(window.at[:, rows, cols(core, c)], spread[c].at[mine], P1 + c, (to, core)).start()
    kept = []
    for c in range(CHUNKS):
        rows = pl.ds(pl.multiple_of(strip * SLIVER, SLIVER), SLIVER)
        kept.append(pltpu.make_async_copy(window.at[:, rows, cols(me, c)], spread[c].at[mine], local_sem.at[P1 + c]))
        kept[c].start()
        drain.append(many(93, P1 + c))


    load_ids.wait()
    lanes = lax.broadcasted_iota(jnp.int32, (8, SLOTS), 1)

    def seat(slot, seats):
        return jnp.where(lanes == ids[slot], slot, seats)

    table[...] = lax.fori_loop(0, SLOTS, seat, jnp.zeros((8, SLOTS), jnp.int32), unroll=8)
    fetch = pltpu.make_async_copy(table, places, load_sem.at[7])
    fetch.start()

    pl.semaphore_wait(ready_sem.at[2], 3)

    def pick(c):
        many(93, P1 + c).wait_recv()
        kept[c].wait()

        def one(slot, _):
            held = ids[slot]
            routed[c, slot] = spread[c][jnp.where(held < 0, BLOCKS, held)]
            return 0

        lax.fori_loop(0, SLOTS, one, 0, unroll=8)

    arrivals = {}

    def route(c, s):
        for offset in cube_order():
            to, _, _ = chip(offset)
            remote(routed.at[c, 2 * to + s], block.at[s, my_rows, cols(me, c)], P2 + s, (to, me)).start()
        arrivals[c, s] = pltpu.make_async_copy(
            routed.at[c, 2 * dp + s], block.at[s, my_rows, cols(me, c)], local_sem.at[2 * CHUNKS + 2 * c + s]
        )
        arrivals[c, s].start()

    for c in range(CHUNKS):
        pick(c)
        route(c, 0)
        if c == 0:
            load_left.wait()
            send_left = remote(left.at[:, my_half, :], left.at[:, my_half, :], LX, (dp, other))
            send_left.start()
            drain.append(send_left)
    for c in range(CHUNKS):
        route(c, 1)
    fetch.wait()
    drain += [slot_copies(s) for s in range(2)]

    own = pl.ds(pl.multiple_of(me * HALF, HALF), HALF)
    exchanges = []

    def arrive(s):
        slot_copies(s).wait_recv()
        for c in range(CHUNKS):
            arrivals[c, s].wait()
        send_block = remote(block.at[s, :, own], block.at[s, :, own], GX + s, (dp, other))
        send_block.start()
        exchanges.append(send_block)
        drain.append(send_block)
        if s == 0:
            send_left.wait_recv()

        def left_tile(r, _):
            rows = pl.ds(pl.multiple_of(r * 256, 256), 256)
            part[s, rows, own] = jnp.dot(
                left[s, rows, :], block[s, :, own], preferred_element_type=jnp.float32
            ).astype(jnp.bfloat16)
            return 0

        lax.fori_loop(0, 4, left_tile, 0)
        send_part = remote(part.at[s, :, own], part.at[s, :, own], PX + s, (dp, other))
        send_part.start()
        drain.append(send_part)
        return send_part

    homes = {}

    def give_back(s, c):
        def dir_tile(r, _):
            rows = pl.ds(pl.multiple_of(r * 256, 256), 256)
            result[s, rows, pl.ds(c * W, W)] = jnp.dot(
                part[s, rows, :], right[s, :, pl.ds(c * W, W)], preferred_element_type=jnp.float32
            ).astype(jnp.bfloat16)
            return 0

        lax.fori_loop(0, 4, dir_tile, 0)
        for offset in cube_order():
            to, to_strip, to_x = chip(offset)
            rows = pl.ds(pl.multiple_of(to_x * QUARTER + to_strip * SLIVER, SLIVER), SLIVER)
            remote(result.at[s, rows, pl.ds(c * W, W)], back[c].at[2 * dp + s], P3 + c, (to, me)).start()
        homes[c, s] = pltpu.make_async_copy(
            result.at[s, my_rows, pl.ds(c * W, W)], back[c].at[2 * dp + s], local_sem.at[4 * CHUNKS + 2 * c + s]
        )
        homes[c, s].start()

    load_right.wait()
    def gram(s, i, total, axis):
        r, n = i // 2, i % 2
        rows = pl.ds(pl.multiple_of(r * 256, 256), 256)
        here = pl.ds(pl.multiple_of(me * HALF + r * 256, 256), 256)
        to = pl.ds(pl.multiple_of(n * 512, 512), 512)
        pair = (block[s, here, :], block[s, to, :]) if axis else (block[s, :, here], block[s, :, to])
        product = lax.dot_general(*pair, (((axis,), (axis,)), ((), ())), preferred_element_type=jnp.float32)
        total[s, rows, to] = KEEP * total[s, rows, to] + (1.0 - KEEP) * product

    def grams(s):
        def both(i, _):
            gram(s, i, new_left, 1)
            gram(s, i, new_right, 0)
            return 0

        lax.fori_loop(0, 4, both, 0)

    for s in range(2):
        arrive(s).wait_recv()
        for c in range(CHUNKS):
            give_back(s, c)
        exchanges[s].wait_recv()
        if s == 0:
            load_sl.wait()
            load_sr.wait()
        grams(s)
    drain += [many(126, P3 + c) for c in range(CHUNKS)]

    ends = []
    for c in range(CHUNKS):
        many(126, P3 + c).wait_recv()
        for s in range(2):
            homes[c, s].wait()

        def choose(b, _):
            chosen[c, b] = back[c][places[0, b]]
            return 0

        lax.fori_loop(0, BLOCKS, choose, 0, unroll=8)
        rows = pl.ds(pl.multiple_of(strip * SLIVER, SLIVER), SLIVER)
        for offset in DIAGONALS + LINES + [(0, 0, 0)]:
            to, to_strip, _ = chip(offset)
            for core in (me, other):
                for j in range(3):
                    src = chosen.at[c, to_strip * 6 + core * 3 + j]
                    dst = direction.at[rows, pl.ds(pl.multiple_of(j * BS + me * HALF + c * W, 128), W)]
                    if any(offset) or core is other:
                        remote(src, dst, P4 + c, (to, core)).start()
                    else:
                        ends.append(pltpu.make_async_copy(src, dst, local_sem.at[6 * CHUNKS + 3 * c + j]))
                        ends[-1].start()
        drain.append(many(93, P4 + c))
    for c in range(CHUNKS):
        many(93, P4 + c).wait_recv()
    for end in ends:
        end.wait()
    for copy in drain:
        copy.wait_send()


def write(a, b, c, a_out, b_out, c_out, sem):
    pairs = [(b, b_out), (c, c_out), (a, a_out)]
    copies = [pltpu.make_async_copy(src, dst, sem.at[i]) for i, (src, dst) in enumerate(pairs)]
    for copy in copies:
        copy.start()
    for copy in copies:
        copy.wait()


def on_device(grads, slot_block, left_stats, right_stats, left_root, right_root):
    bf16 = jnp.bfloat16
    anywhere = pl.BlockSpec(memory_space=pl.ANY)
    outs = [(grads.shape, bf16), (left_stats.shape, jnp.float32), (right_stats.shape, jnp.float32)]
    results = pl.pallas_call(
        kernel,
        out_shape=[pltpu.VMEM(*out) for out in outs],
        in_specs=[anywhere] * 6,
        out_specs=[pl.BlockSpec(memory_space=pltpu.VMEM)] * 3,
        scratch_shapes=[
            pltpu.VMEM((3, QUARTER, BS), bf16),
            [pltpu.VMEM((BLOCKS + 1, SLIVER, W), bf16) for _ in range(CHUNKS)],
            pltpu.VMEM((CHUNKS, SLOTS, SLIVER, W), bf16),
            pltpu.VMEM((2, BS, BS), bf16),
            pltpu.VMEM((2, BS, BS), bf16),
            pltpu.VMEM((2, BS, HALF), bf16),
            pltpu.VMEM((2, BS, BS), bf16),
            pltpu.VMEM((2, BS, HALF), bf16),
            [pltpu.VMEM((SLOTS, SLIVER, W), bf16) for _ in range(CHUNKS)],
            pltpu.VMEM((CHUNKS, BLOCKS, SLIVER, W), bf16),
            pltpu.VMEM((8, SLOTS), jnp.int32),
            pltpu.SMEM((8, SLOTS), jnp.int32),
            pltpu.SMEM((SLOTS,), jnp.int32),
            pltpu.SemaphoreType.DMA((9,)),
            pltpu.SemaphoreType.DMA((9 * CHUNKS,)),
            pltpu.SemaphoreType.DMA((3 * CHUNKS + 7,)),
            pltpu.SemaphoreType.DMA((3 * CHUNKS + 7,)),
            pltpu.SemaphoreType.REGULAR((3,)),
        ],
        compiler_params=pltpu.CompilerParams(
            collective_id=0, has_side_effects=True, vmem_limit_bytes=50 * 2**20
        ),
    )(slot_block, grads, left_stats, right_stats, left_root, right_root)
    return pl.pallas_call(
        write,
        out_shape=[jax.ShapeDtypeStruct(*out) for out in outs],
        in_specs=[anywhere] * 3,
        out_specs=[anywhere] * 3,
        scratch_shapes=[pltpu.SemaphoreType.DMA((3,))],
        compiler_params=pltpu.CompilerParams(vmem_limit_bytes=2**20),
    )(*results)


def solution(mesh):
    return jax.shard_map(
        on_device,
        mesh=mesh,
        in_specs=(
            P("dp", "mp"),
            P(),
            P("dp", "mp", None),
            P("dp", "mp", None),
            P("dp", "mp", None),
            P("dp", None, "mp"),
        ),
        out_specs=(P("dp", "mp"), P("dp", "mp", None), P("dp", "mp", None)),
        check_vma=False,
    )
```
